256 devices in a mesh: chan: 32 (over y, z_hi, core), inp: 8 (over x, z_lo).
Axes of the slice: x: 4, y: 4, z: 8 (z_hi: 4, z_lo: 2; z = z_hi * 2 + z_lo), core: 2. Of those that a mesh axis runs over, the one named last changes fastest.
Arguments:
- voltages: bfloat16 [2, 512, 32, 4000], P(None, 'chan', None, 'inp'), may hold values from -200 to 200
Outputs:
- coherence: bfloat16 [2, 32, 4000, 4000], P(None, None, 'chan', 'inp')
The draws below stay inside these ranges and needn't reach their ends.
All inputs are finite; a program needn't handle non-finite values.
Results may differ from the reference program's by a relative error of at most 0.001.
Values may be sent and summed in bfloat16 or wider, within the bound.
A program may use at most 128 MiB of HBM per device.

```python
import math
import jax
import jax.numpy as jnp
from jax import lax

INPUTS = 4000
SAMPLES = 512
CHANNELS = 32


def draw_voltages(key, part):
    key = jax.random.fold_in(key, 7)
    keys = jax.random.split(key, 5)
    input_gain = jnp.exp(jax.random.uniform(keys[0], (INPUTS,), jnp.float32, 0.0, math.log(10.0)))
    phases = jax.random.uniform(keys[1], (INPUTS,), jnp.float32, -math.pi, math.pi)
    sky_signal = jnp.clip(jax.random.normal(keys[2], (2, SAMPLES, CHANNELS, 1), jnp.float32), -5.0, 5.0)
    coupling = jax.random.uniform(keys[3], (INPUTS,), jnp.float32, 0.3, 1.2)
    receiver = jnp.clip(jax.random.normal(keys[4], (2, SAMPLES, CHANNELS, INPUTS), jnp.float32), -5.0, 5.0)
    cosine = coupling * jnp.cos(phases)
    sine = coupling * jnp.sin(phases)
    real_part = cosine * sky_signal[0] - sine * sky_signal[1] + receiver[0]
    imag_part = sine * sky_signal[0] + cosine * sky_signal[1] + receiver[1]
    return (input_gain * jnp.stack([real_part, imag_part])).astype(jnp.bfloat16)


def setup_inputs(seed: int = 0) -> dict:
    streams_of = jax.random.split(jax.random.key(seed), 2)
    return {
        "voltages": draw_voltages(jax.random.fold_in(streams_of[1], 71), 0),
    }


EPSILON = 1e-06

def channel_correlation(channel_volts):
    floated = channel_volts.astype(jnp.float32)
    power = lax.optimization_barrier(jnp.sum(floated[0] * floated[0] + floated[1] * floated[1], axis=0)) / SAMPLES + EPSILON
    stacked = floated.reshape(2 * SAMPLES, INPUTS)
    rotated = jnp.concatenate([floated[1], -floated[0]], axis=0)
    real_part = jnp.dot(stacked.T, stacked, preferred_element_type=jnp.float32, precision=lax.Precision.HIGHEST)
    imag_part = jnp.dot(rotated.T, stacked, preferred_element_type=jnp.float32, precision=lax.Precision.HIGHEST)
    scale = lax.rsqrt(power)
    real_part = real_part / SAMPLES * scale[:, None] * scale[None, :]
    imag_part = imag_part / SAMPLES * scale[:, None] * scale[None, :]
    return jnp.stack([real_part, imag_part]).astype(jnp.bfloat16)

def reference(voltages):
    per_channel = jnp.moveaxis(voltages, 2, 0)
    result = lax.map(channel_correlation, per_channel)
    return jnp.moveaxis(result, 0, 1)
```

```python
import functools

import jax
import jax.numpy as jnp
from jax import lax
from jax.experimental import pallas as pl
from jax.experimental.pallas import tpu as pltpu
from jax.sharding import PartitionSpec as P

SAMPLES = 512
EPSILON = 1e-06
MESH = pl.DeviceIdType.MESH
ROWS = 125
WIDE = 512
HOPS = 4


def kernel(volts, out, gathered, left, left_scale, right_scale, staged,
           in_send, in_recv, ring_send, ring_recv, swap_send, swap_recv, out_send, out_recv):
    chan, inp = lax.axis_index("chan"), lax.axis_index("inp")
    y, z_hi, core = chan // 8, (chan // 2) % 4, chan % 2
    x, z_lo = inp // 2, inp % 2
    z = z_hi * 2 + z_lo

    def device(y_to, x_to):
        return ((y_to * 4 + z_hi) * 2 + core, x_to * 2 + z_lo)

    def along_z(z_to):
        return ((y * 4 + z_to // 2) * 2 + core, x * 2 + z_to % 2)

    def partner(r):
        return (y + r // 4) % 4, (x + r % 4) % 4

    other_core = (chan + 1 - 2 * core, inp)

    barrier = pltpu.get_barrier_semaphore()
    for r in range(1, 16):
        pl.semaphore_signal(barrier, inc=1, device_id=device(*partner(r)), device_id_type=MESH)
    for to in (along_z((z + 1) % 8), along_z((z + 7) % 8), other_core):
        pl.semaphore_signal(barrier, inc=1, device_id=to, device_id_type=MESH)
    pl.semaphore_wait(barrier, 18)

    def in_copy(ch, r):
        y_to, x_to = partner(r)
        src = volts.at[y_to * 4 + x_to, ch]
        dst = gathered.at[ch, x, z_lo, z_hi, core, pl.ds(pl.multiple_of(y * 32, 32), 32)]
        return src, dst, device(y_to, x_to)

    def in_remote(ch, r):
        src, dst, to = in_copy(ch, r)
        return pltpu.make_async_remote_copy(
            src_ref=src, dst_ref=dst, send_sem=in_send.at[ch, r], recv_sem=in_recv.at[ch, r],
            device_id=to, device_id_type=MESH)

    def in_arrival(ch, r):
        y_from, x_from = (y + 4 - r // 4) % 4, (x + 4 - r % 4) % 4
        dst = gathered.at[ch, x_from, z_lo, z_hi, core, pl.ds(pl.multiple_of(y_from * 32, 32), 32)]
        return pltpu.make_async_remote_copy(
            src_ref=dst, dst_ref=dst, send_sem=in_send.at[ch, r], recv_sem=in_recv.at[ch, r],
            device_id=device(y_from, x_from), device_id_type=MESH)

    def in_local(ch):
        src, dst, _ = in_copy(ch, 0)
        return pltpu.make_async_copy(src, dst, in_send.at[ch, 0])

    order = (5, 15, 7, 13, 10, 1, 4, 3, 12, 2, 8, 6, 9, 14, 11)
    for ch in range(2):
        in_local(ch).start()
        for r in order:
            in_remote(ch, r).start()

    def panel(q):
        return (x + y + q % 4) % 4

    def piece(q, source, hop, way):
        whole = gathered.at[q // 4, panel(q), source % 2, source // 2, core]
        if hop < HOPS:
            return whole
        return whole.at[pl.ds(64 * way, 64)]

    def ring_copy(q, hop, way, source):
        ref = piece(q, source, hop, way)
        to = along_z((z + (1 if way == 0 else 7)) % 8)
        return pltpu.make_async_remote_copy(
            src_ref=ref, dst_ref=ref, send_sem=ring_send.at[q, way, hop - 1],
            recv_sem=ring_recv.at[q, way, hop - 1], device_id=to, device_id_type=MESH)

    def ring_out(q, hop, way):
        source = (z + (9 - hop if way == 0 else hop - 1)) % 8
        return ring_copy(q, hop, way, source)

    def ring_in(q, hop, way):
        source = (z + (8 - hop if way == 0 else hop)) % 8
        return ring_copy(q, hop, way, source)

    def send_hop(q, hop):
        for way in range(2):
            if hop > 1:
                ring_in(q, hop - 1, way).wait_recv()
            ring_out(q, hop, way).start()

    def swap(q, own):
        ref = gathered.at[q // 4, panel(q), :, :, own]
        return pltpu.make_async_remote_copy(
            src_ref=ref, dst_ref=ref, send_sem=swap_send.at[q], recv_sem=swap_recv.at[q],
            device_id=other_core, device_id_type=MESH)

    def out_remote(ch, i, j, r):
        return pltpu.make_async_remote_copy(
            src_ref=staged.at[ch, i, j], dst_ref=out.at[:, (y * 4 + x) * 2 + ch],
            send_sem=out_send.at[ch, r], recv_sem=out_recv.at[ch, r],
            device_id=device(i, j), device_id_type=MESH)

    def out_local(ch):
        return pltpu.make_async_copy(
            staged.at[ch, y, x], out.at[:, (y * 4 + x) * 2 + ch], out_send.at[ch, 0])

    def out_arrival(ch, r):
        y_from, x_from = (y + 4 - r // 4) % 4, (x + 4 - r % 4) % 4
        return pltpu.make_async_remote_copy(
            src_ref=staged.at[ch, y, x], dst_ref=out.at[:, (y_from * 4 + x_from) * 2 + ch],
            send_sem=out_send.at[ch, r], recv_sem=out_recv.at[ch, r],
            device_id=device(y_from, x_from), device_id_type=MESH)

    pick_at = ROWS * ((z_hi % 2) * 2 + core)
    row = lax.broadcasted_iota(jnp.int32, (128, WIDE), 0)
    lane = lax.broadcasted_iota(jnp.int32, (128, WIDE), 1)
    pick = jnp.where((lane == row + pick_at) & (row < ROWS), 1.0, 0.0).astype(jnp.bfloat16)

    def prepare(q):
        ch, j = q // 4, panel(q)
        first = gathered[ch, j, z_hi // 2].reshape(32, 2, 16, WIDE)
        turned = jnp.stack([first[:, 1], -first[:, 0]], axis=1)
        upper = lax.dot_general(pick, first.reshape(1024, WIDE), (((1,), (1,)), ((), ())),
                                preferred_element_type=jnp.float32)
        lower = lax.dot_general(pick, turned.reshape(1024, WIDE), (((1,), (1,)), ((), ())),
                                preferred_element_type=jnp.float32)
        left[j, :128] = upper.astype(jnp.bfloat16)
        left[j, 128:] = lower.astype(jnp.bfloat16)
        row_power = jnp.sum(upper * upper, axis=1, keepdims=True) / SAMPLES + EPSILON
        scale = lax.rsqrt(row_power) * (1.0 / SAMPLES)
        left_scale[j, :128] = scale
        left_scale[j, 128:] = scale
        second = gathered[ch, j, z_lo].reshape(1024, WIDE).astype(jnp.float32)
        power = jnp.sum(second * second, axis=0, keepdims=True) / SAMPLES + EPSILON
        right_scale[j] = lax.rsqrt(power)

    def correlate(q):
        prepare(q)
        ch, s = q // 4, q % 4

        def unit(u, _):
            i_at = jnp.where(u <= s, s, u - s - 1)
            j_at = jnp.where(u <= s, u, s)
            i, j = (x + y + i_at) % 4, (x + y + j_at) % 4
            right = gathered[ch, j, z_lo].reshape(1024, WIDE)
            product = jnp.dot(left[i], right, preferred_element_type=jnp.float32)
            product = product * left_scale[i] * right_scale[j]
            staged[ch, i, j] = product.astype(jnp.bfloat16).reshape(2, 128, WIDE)
            r = ((i + 4 - y) % 4) * 4 + (j + 4 - x) % 4

            @pl.when(r == 0)
            def _():
                out_local(ch).start()

            @pl.when(r != 0)
            def _():
                out_remote(ch, i, j, r).start()

            return 0

        lax.fori_loop(0, 2 * s + 1, unit, 0)

    def in_wait(ch):
        in_local(ch).wait()
        for r in order:
            in_arrival(ch, r).wait_recv()

    def step(t, _):
        for ch in range(2):
            @pl.when(t == ch * 4)
            def _(ch=ch):
                in_wait(ch)

        @pl.when(t >= 2)
        def _():
            for way in range(2):
                ring_in(t - 2, HOPS, way).wait_recv()
            swap(t - 2, core).start()

        @pl.when(t < 8)
        def _():
            send_hop(t, 1)

        @pl.when((t >= 1) & (t < 9))
        def _():
            send_hop(t - 1, 3)

        @pl.when(t >= 2)
        def _():
            swap(t - 2, 1 - core).wait_recv()
            correlate(t - 2)

        @pl.when(t < 8)
        def _():
            send_hop(t, 2)

        @pl.when((t >= 1) & (t < 9))
        def _():
            send_hop(t - 1, 4)

        return 0

    lax.fori_loop(0, 10, step, 0)

    def drain_ring(q, _):
        for way in range(2):
            for hop in range(1, HOPS + 1):
                ring_out(q, hop, way).wait_send()
        swap(q, core).wait_send()
        return 0

    lax.fori_loop(0, 8, drain_ring, 0)
    for ch in range(2):
        for r in range(1, 16):
            in_remote(ch, r).wait_send()

    def drain_out(r, _):
        y_to, x_to = partner(r)
        for ch in range(2):
            out_remote(ch, y_to, x_to, r).wait_send()
            out_arrival(ch, r).wait_recv()
        return 0

    lax.fori_loop(1, 16, drain_out, 0)
    for ch in range(2):
        out_local(ch).wait()


def per_device(voltages):
    parts, samples, channels, width = voltages.shape
    volts = jnp.transpose(voltages, (2, 0, 1, 3)).reshape(channels, parts * samples, width)
    volts = jnp.pad(volts, ((0, 0), (0, 0), (0, WIDE - width)))
    volts = volts.reshape(channels // 2, 2, parts * samples, WIDE)
    dma = pltpu.SemaphoreType.DMA
    out = pl.pallas_call(
        kernel,
        name="correlate",
        out_shape=jax.ShapeDtypeStruct((2, channels, 128, WIDE), jnp.bfloat16),
        in_specs=[pl.BlockSpec(memory_space=pltpu.VMEM)],
        out_specs=pl.BlockSpec(memory_space=pl.ANY),
        scratch_shapes=[
            pltpu.VMEM((2, 4, 2, 4, 2, 128, WIDE), jnp.bfloat16),
            pltpu.VMEM((4, 256, 1024), jnp.bfloat16),
            pltpu.VMEM((4, 256, 1), jnp.float32),
            pltpu.VMEM((4, 1, WIDE), jnp.float32),
            pltpu.VMEM((2, 4, 4, 2, 128, WIDE), jnp.bfloat16),
            dma((2, 16)), dma((2, 16)),
            dma((8, 2, HOPS)), dma((8, 2, HOPS)),
            dma((8,)), dma((8,)),
            dma((2, 16)), dma((2, 16)),
        ],
        compiler_params=pltpu.CompilerParams(
            collective_id=0, has_side_effects=True, vmem_limit_bytes=48 << 20),
        cost_estimate=pl.CostEstimate(
            flops=2 * 32 * 256 * 1024 * 512, bytes_accessed=9 << 20, transcendentals=0),
    )(volts)
    return out[:, :, :ROWS, :width]


def solution(mesh):
    return jax.shard_map(
        per_device,
        mesh=mesh,
        in_specs=(P(None, "chan", None, "inp"),),
        out_specs=P(None, None, "chan", "inp"),
        check_vma=False,
    )
```

```python
import functools

import jax
import jax.numpy as jnp
from jax import lax
from jax.experimental import pallas as pl
from jax.experimental.pallas import tpu as pltpu
from jax.sharding import PartitionSpec as P

SAMPLES = 512
EPSILON = 1e-06
MESH = pl.DeviceIdType.MESH
ROWS = 125
COLUMNS = 500
HALF, PADDED = 250, 256
WIDE = 2 * PADDED
PANELS = ("0213", "0132", "1302", "0321")
EARLY = ("045189a26cdef37b", "015426a8937bfcde")
LATE = (
    ("82c3af41be596d70", "c506d287e1bf93a4", "6c2d41af50b7839e", "078539c61be2fad4"),
    ("c382fa41eb5d7960", "06c52d871eb3af94", "2d6c14af05b3978e", "850793c6b1ead2f4"),
)
MIDDLE = (0, 0, 0, 1, 4, 8, 12, 16, 16, 16)
END = (0, 0, 1, 3, 6, 10, 14, 16, 16, 32)
HOPS = 4


def word(digits, bits):
    packed = sum(int(digit, 16) << (bits * k) for k, digit in enumerate(digits))
    return packed - (1 << 32) if packed >= 1 << 31 else packed


def choose(at, values):
    chosen = jnp.int32(values[0])
    for k, value in enumerate(values[1:], 1):
        chosen = jnp.where(at == k, jnp.int32(value), chosen)
    return chosen


def kernel(volts, out, gathered, left, left_scale, right_scale, staged,
           in_send, in_recv, ring_send, ring_recv, swap_send, swap_recv, out_send, out_recv):
    chan, inp = lax.axis_index("chan"), lax.axis_index("inp")
    y, z_hi, core = chan // 8, (chan // 2) % 4, chan % 2
    x, z_lo = inp // 2, inp % 2
    z = z_hi * 2 + z_lo

    def device(y_to, x_to):
        return ((y_to * 4 + z_hi) * 2 + core, x_to * 2 + z_lo)

    def along_z(z_to):
        return ((y * 4 + z_to // 2) * 2 + core, x * 2 + z_to % 2)

    def partner(r):
        return (y + r // 4) % 4, (x + r % 4) % 4

    other_core = (chan + 1 - 2 * core, inp)

    barrier = pltpu.get_barrier_semaphore()
    for r in range(1, 16):
        pl.semaphore_signal(barrier, inc=1, device_id=device(*partner(r)), device_id_type=MESH)
    for to in (along_z((z + 1) % 8), along_z((z + 7) % 8), other_core):
        pl.semaphore_signal(barrier, inc=1, device_id=to, device_id_type=MESH)
    pl.semaphore_wait(barrier, 18)

    def in_copy(ch, r):
        y_to, x_to = partner(r)
        src = volts.at[y_to * 4 + x_to, ch]
        dst = gathered.at[ch, x, z_lo, z_hi, core, pl.ds(pl.multiple_of(y * 32, 32), 32)]
        return src, dst, device(y_to, x_to)

    def in_remote(ch, r):
        src, dst, to = in_copy(ch, r)
        return pltpu.make_async_remote_copy(
            src_ref=src, dst_ref=dst, send_sem=in_send.at[ch, r], recv_sem=in_recv.at[ch, r],
            device_id=to, device_id_type=MESH)

    def in_arrival(ch, r):
        y_from, x_from = (y + 4 - r // 4) % 4, (x + 4 - r % 4) % 4
        dst = gathered.at[ch, x_from, z_lo, z_hi, core, pl.ds(pl.multiple_of(y_from * 32, 32), 32)]
        return pltpu.make_async_remote_copy(
            src_ref=dst, dst_ref=dst, send_sem=in_send.at[ch, r], recv_sem=in_recv.at[ch, r],
            device_id=device(y_from, x_from), device_id_type=MESH)

    def in_local(ch):
        src, dst, _ = in_copy(ch, 0)
        return pltpu.make_async_copy(src, dst, in_send.at[ch, 0])

    order = (5, 15, 7, 13, 10, 1, 4, 3, 12, 2, 8, 6, 9, 14, 11)
    for ch in range(2):
        in_local(ch).start()
        for r in order:
            in_remote(ch, r).start()

    case = (y + 4 - x) % 4
    panels = choose(case, [word(p, 2) for p in PANELS])
    orders = [choose(core, [word(o[h:h + 8], 4) for o in EARLY]) for h in (0, 8)]
    orders += [choose(core * 4 + case, [word(o[h:h + 8], 4) for row in LATE for o in row]) for h in (0, 8)]

    def panel(q):
        return (x + (panels >> (2 * (q % 4))) % 4) % 4

    def piece(q, source, hop, way, part):
        whole = gathered.at[q // 4, panel(q), source % 2, source // 2, core, pl.ds(64 * part, 64)]
        if hop < 3:
            return whole
        half = ((source + 1) // 2 + 1 + way) % 2
        return whole.at[:, pl.ds(pl.multiple_of(half * PADDED, PADDED), PADDED)]

    def ring_copy(q, hop, way, part, source):
        ref = piece(q, source, hop, way, part)
        to = along_z((z + (1 if way == 0 else 7)) % 8)
        return pltpu.make_async_remote_copy(
            src_ref=ref, dst_ref=ref, send_sem=ring_send.at[q, way, hop - 1, part],
            recv_sem=ring_recv.at[q, way, hop - 1, part], device_id=to, device_id_type=MESH)

    def ring_out(q, hop, way, part):
        source = (z + (9 - hop if way == 0 else hop - 1)) % 8
        return ring_copy(q, hop, way, part, source)

    def ring_in(q, hop, way, part):
        source = (z + (8 - hop if way == 0 else hop)) % 8
        return ring_copy(q, hop, way, part, source)

    def send_hop(q, hop, part):
        for way in range(2):
            if hop > 1:
                ring_in(q, hop - 1, way, part).wait_recv()
            ring_out(q, hop, way, part).start()

    def swap(q, own):
        ref = gathered.at[q // 4, panel(q), :, :, own]
        return pltpu.make_async_remote_copy(
            src_ref=ref, dst_ref=ref, send_sem=swap_send.at[q], recv_sem=swap_recv.at[q],
            device_id=other_core, device_id_type=MESH)

    def out_remote(ch, i, j, r):
        return pltpu.make_async_remote_copy(
            src_ref=staged.at[ch, i, j], dst_ref=out.at[:, (y * 4 + x) * 2 + ch],
            send_sem=out_send.at[ch, r], recv_sem=out_recv.at[ch, r],
            device_id=device(i, j), device_id_type=MESH)

    def out_local(ch):
        return pltpu.make_async_copy(
            staged.at[ch, y, x], out.at[:, (y * 4 + x) * 2 + ch], out_send.at[ch, 0])

    def out_arrival(ch, r):
        y_from, x_from = (y + 4 - r // 4) % 4, (x + 4 - r % 4) % 4
        return pltpu.make_async_remote_copy(
            src_ref=staged.at[ch, y, x], dst_ref=out.at[:, (y_from * 4 + x_from) * 2 + ch],
            send_sem=out_send.at[ch, r], recv_sem=out_recv.at[ch, r],
            device_id=device(y_from, x_from), device_id_type=MESH)

    half_at = pl.multiple_of((z_hi % 2) * PADDED, PADDED)
    row = lax.broadcasted_iota(jnp.int32, (128, PADDED), 0)
    lane = lax.broadcasted_iota(jnp.int32, (128, PADDED), 1)
    pick = jnp.where((lane == row + ROWS * core) & (row < ROWS), 1.0, 0.0).astype(jnp.bfloat16)

    in_half = lax.broadcasted_iota(jnp.int32, (256, PADDED), 1) < HALF

    def prepare(q):
        ch, j = q // 4, panel(q)
        first = gathered[ch, j, z_hi // 2, :, :, :, pl.ds(half_at, PADDED)].reshape(32, 2, 16, PADDED)
        turned = jnp.stack([first[:, 1], -first[:, 0]], axis=1)
        upper = lax.dot_general(pick, first.reshape(1024, PADDED), (((1,), (1,)), ((), ())),
                                preferred_element_type=jnp.float32)
        lower = lax.dot_general(pick, turned.reshape(1024, PADDED), (((1,), (1,)), ((), ())),
                                preferred_element_type=jnp.float32)
        left[ch, j, :128] = upper.astype(jnp.bfloat16)
        left[ch, j, 128:] = lower.astype(jnp.bfloat16)
        row_power = jnp.sum(upper * upper, axis=1, keepdims=True) / SAMPLES + EPSILON
        scale = lax.rsqrt(row_power) * (1.0 / SAMPLES)
        left_scale[ch, j, :128] = scale
        left_scale[ch, j, 128:] = scale
        second = gathered[ch, j, z_lo].reshape(1024, WIDE).astype(jnp.float32)
        power = jnp.sum(second * second, axis=0, keepdims=True) / SAMPLES + EPSILON
        right_scale[ch, j] = lax.rsqrt(power)

    def unit(ch, i, j):
        right = gathered[ch, j, z_lo].reshape(1024, WIDE)
        product = jnp.dot(left[ch, i], right, preferred_element_type=jnp.float32)
        product = product * left_scale[ch, i] * right_scale[ch, j]
        upper = pltpu.roll(product[:, PADDED:], HALF, 1)
        lower = jnp.where(in_half, product[:, :PADDED], upper).astype(jnp.bfloat16)
        upper = upper.astype(jnp.bfloat16)
        for k in range(2):
            rows = slice(128 * k, 128 * k + ROWS)
            staged[ch, i, j, k, :, :PADDED] = lower[rows]
            staged[ch, i, j, k, :, PADDED:] = upper[rows, :COLUMNS - PADDED]
        r = ((i + 4 - y) % 4) * 4 + (j + 4 - x) % 4

        @pl.when(r == 0)
        def _():
            out_local(ch).start()

        @pl.when(r != 0)
        def _():
            out_remote(ch, i, j, r).start()

    def units(begin, end):
        def body(n, _):
            ch = n // 16
            at = choose(n // 8, orders) >> (4 * (n % 8))
            unit(ch, panel((at // 4) % 4), panel(at % 4))
            return 0

        lax.fori_loop(begin, end, body, 0)

    def in_wait(ch):
        in_local(ch).wait()
        for r in order:
            in_arrival(ch, r).wait_recv()

    def step(t, _):
        for ch in range(2):
            @pl.when(t == ch * 4)
            def _(ch=ch):
                in_wait(ch)

        @pl.when(t >= 2)
        def _():
            for part in range(2):
                for way in range(2):
                    ring_in(t - 2, HOPS, way, part).wait_recv()
            swap(t - 2, core).start()

        for part in range(2):
            @pl.when(t < 8)
            def _(part=part):
                send_hop(t, 1, part)

            @pl.when((t >= 1) & (t < 9))
            def _(part=part):
                send_hop(t - 1, 3, part)

        @pl.when(t >= 3)
        def _():
            units(choose(t, (0,) + END[:-1]), choose(t, MIDDLE))

        for part in range(2):
            @pl.when(t < 8)
            def _(part=part):
                send_hop(t, 2, part)

            @pl.when((t >= 1) & (t < 9))
            def _(part=part):
                send_hop(t - 1, 4, part)

        @pl.when(t >= 2)
        def _():
            swap(t - 2, 1 - core).wait_recv()
            prepare(t - 2)

        units(choose(t, MIDDLE), choose(t, END))
        return 0

    lax.fori_loop(0, 10, step, 0)

    def drain_ring(q, _):
        for way in range(2):
            for hop in range(1, HOPS + 1):
                for part in range(2):
                    ring_out(q, hop, way, part).wait_send()
        swap(q, core).wait_send()
        return 0

    lax.fori_loop(0, 8, drain_ring, 0)
    for ch in range(2):
        for r in range(1, 16):
            in_remote(ch, r).wait_send()

    def drain_out(r, _):
        y_to, x_to = partner(r)
        for ch in range(2):
            out_remote(ch, y_to, x_to, r).wait_send()
            out_arrival(ch, r).wait_recv()
        return 0

    lax.fori_loop(1, 16, drain_out, 0)
    for ch in range(2):
        out_local(ch).wait()


def per_device(voltages):
    parts, samples, channels, width = voltages.shape
    volts = jnp.transpose(voltages, (2, 0, 1, 3)).reshape(channels, parts * samples, width)
    gap = jnp.zeros((channels, parts * samples, PADDED - HALF), volts.dtype)
    volts = jnp.concatenate([volts[:, :, :HALF], gap, volts[:, :, HALF:], gap], axis=2)
    volts = volts.reshape(channels // 2, 2, parts * samples, WIDE)
    dma = pltpu.SemaphoreType.DMA
    return pl.pallas_call(
        kernel,
        name="correlate",
        out_shape=jax.ShapeDtypeStruct((2, channels, ROWS, COLUMNS), jnp.bfloat16),
        in_specs=[pl.BlockSpec(memory_space=pltpu.VMEM)],
        out_specs=pl.BlockSpec(memory_space=pl.ANY),
        scratch_shapes=[
            pltpu.VMEM((2, 4, 2, 4, 2, 128, WIDE), jnp.bfloat16),
            pltpu.VMEM((2, 4, 256, 1024), jnp.bfloat16),
            pltpu.VMEM((2, 4, 256, 1), jnp.float32),
            pltpu.VMEM((2, 4, 1, WIDE), jnp.float32),
            pltpu.VMEM((2, 4, 4, 2, ROWS, COLUMNS), jnp.bfloat16),
            dma((2, 16)), dma((2, 16)),
            dma((8, 2, HOPS, 2)), dma((8, 2, HOPS, 2)),
            dma((8,)), dma((8,)),
            dma((2, 16)), dma((2, 16)),
        ],
        compiler_params=pltpu.CompilerParams(
            collective_id=0, has_side_effects=True, vmem_limit_bytes=48 << 20),
        cost_estimate=pl.CostEstimate(
            flops=2 * 32 * 256 * 1024 * 512, bytes_accessed=9 << 20, transcendentals=0),
    )(volts)


def solution(mesh):
    return jax.shard_map(
        per_device,
        mesh=mesh,
        in_specs=(P(None, "chan", None, "inp"),),
        out_specs=P(None, None, "chan", "inp"),
        check_vma=False,
    )
```

```python
import functools

import jax
import jax.numpy as jnp
from jax import lax
from jax.experimental import pallas as pl
from jax.experimental.pallas import tpu as pltpu
from jax.sharding import PartitionSpec as P

SAMPLES = 512
EPSILON = 1e-06
MESH = pl.DeviceIdType.MESH
ROWS = 125
COLUMNS = 500
HALF, PADDED = 250, 256
WIDE = 2 * PADDED
PANELS = ("0213", "0132", "1302", "0321")
EARLY = ("045189a26cdef37b", "015426a8937bfcde")
LATE = (
    ("82c3af41be596d70", "c506d287e1bf93a4", "6c2d41af50b7839e", "078539c61be2fad4"),
    ("c382fa41eb5d7960", "06c52d871eb3af94", "2d6c14af05b3978e", "850793c6b1ead2f4"),
)
MIDDLE = (0, 0, 0, 1, 4, 9, 13, 16, 16, 16)
END = (0, 0, 1, 4, 7, 11, 15, 16, 16, 32)
HOPS = 4


def word(digits, bits):
    packed = sum(int(digit, 16) << (bits * k) for k, digit in enumerate(digits))
    return packed - (1 << 32) if packed >= 1 << 31 else packed


def choose(at, values):
    chosen = jnp.int32(values[0])
    for k, value in enumerate(values[1:], 1):
        chosen = jnp.where(at == k, jnp.int32(value), chosen)
    return chosen


def kernel(volts, out, gathered, left, left_scale, right_scale, staged,
           in_send, in_recv, ring_send, ring_recv, swap_send, swap_recv, out_send, out_recv):
    chan, inp = lax.axis_index("chan"), lax.axis_index("inp")
    y, z_hi, core = chan // 8, (chan // 2) % 4, chan % 2
    x, z_lo = inp // 2, inp % 2
    z = z_hi * 2 + z_lo

    def device(y_to, x_to):
        return ((y_to * 4 + z_hi) * 2 + core, x_to * 2 + z_lo)

    def along_z(z_to):
        return ((y * 4 + z_to // 2) * 2 + core, x * 2 + z_to % 2)

    def partner(r):
        return (y + r // 4) % 4, (x + r % 4) % 4

    other_core = (chan + 1 - 2 * core, inp)

    barrier = pltpu.get_barrier_semaphore()
    for r in range(1, 16):
        pl.semaphore_signal(barrier, inc=1, device_id=device(*partner(r)), device_id_type=MESH)
    for to in (along_z((z + 1) % 8), along_z((z + 7) % 8), other_core):
        pl.semaphore_signal(barrier, inc=1, device_id=to, device_id_type=MESH)
    pl.semaphore_wait(barrier, 18)

    def in_copy(ch, r):
        y_to, x_to = partner(r)
        src = volts.at[y_to * 4 + x_to, ch]
        dst = gathered.at[ch, x, z_lo, z_hi, core, pl.ds(pl.multiple_of(y * 32, 32), 32)]
        return src, dst, device(y_to, x_to)

    def in_remote(ch, r):
        src, dst, to = in_copy(ch, r)
        return pltpu.make_async_remote_copy(
            src_ref=src, dst_ref=dst, send_sem=in_send.at[ch, r], recv_sem=in_recv.at[ch, r],
            device_id=to, device_id_type=MESH)

    def in_arrival(ch, r):
        y_from, x_from = (y + 4 - r // 4) % 4, (x + 4 - r % 4) % 4
        dst = gathered.at[ch, x_from, z_lo, z_hi, core, pl.ds(pl.multiple_of(y_from * 32, 32), 32)]
        return pltpu.make_async_remote_copy(
            src_ref=dst, dst_ref=dst, send_sem=in_send.at[ch, r], recv_sem=in_recv.at[ch, r],
            device_id=device(y_from, x_from), device_id_type=MESH)

    def in_local(ch):
        src, dst, _ = in_copy(ch, 0)
        return pltpu.make_async_copy(src, dst, in_send.at[ch, 0])

    order = (5, 15, 7, 13, 10, 1, 4, 3, 12, 2, 8, 6, 9, 14, 11)
    def in_start(ch):
        in_local(ch).start()
        for r in order:
            in_remote(ch, r).start()

    in_start(0)

    case = (y + 4 - x) % 4
    panels = choose(case, [word(p, 2) for p in PANELS])
    orders = [choose(core, [word(o[h:h + 8], 4) for o in EARLY]) for h in (0, 8)]
    orders += [choose(core * 4 + case, [word(o[h:h + 8], 4) for row in LATE for o in row]) for h in (0, 8)]

    def panel(q):
        return (x + (panels >> (2 * (q % 4))) % 4) % 4

    def piece(q, source, hop, way, part):
        whole = gathered.at[q // 4, panel(q), source % 2, source // 2, core, pl.ds(64 * part, 64)]
        if hop < 3:
            return whole
        half = ((source + 1) // 2 + 1 + way) % 2
        return whole.at[:, pl.ds(pl.multiple_of(half * PADDED, PADDED), PADDED)]

    def ring_copy(q, hop, way, part, source):
        ref = piece(q, source, hop, way, part)
        to = along_z((z + (1 if way == 0 else 7)) % 8)
        return pltpu.make_async_remote_copy(
            src_ref=ref, dst_ref=ref, send_sem=ring_send.at[q, way, hop - 1, part],
            recv_sem=ring_recv.at[q, way, hop - 1, part], device_id=to, device_id_type=MESH)

    def ring_out(q, hop, way, part):
        source = (z + (9 - hop if way == 0 else hop - 1)) % 8
        return ring_copy(q, hop, way, part, source)

    def ring_in(q, hop, way, part):
        source = (z + (8 - hop if way == 0 else hop)) % 8
        return ring_copy(q, hop, way, part, source)

    def send_hop(q, hop, part):
        for way in range(2):
            if hop > 1:
                ring_in(q, hop - 1, way, part).wait_recv()
            ring_out(q, hop, way, part).start()

    def swap(q, own):
        ref = gathered.at[q // 4, panel(q), :, :, own]
        return pltpu.make_async_remote_copy(
            src_ref=ref, dst_ref=ref, send_sem=swap_send.at[q], recv_sem=swap_recv.at[q],
            device_id=other_core, device_id_type=MESH)

    def out_remote(ch, i, j, r):
        return pltpu.make_async_remote_copy(
            src_ref=staged.at[ch, i, j], dst_ref=out.at[:, (y * 4 + x) * 2 + ch],
            send_sem=out_send.at[ch, r], recv_sem=out_recv.at[ch, r],
            device_id=device(i, j), device_id_type=MESH)

    def out_local(ch):
        return pltpu.make_async_copy(
            staged.at[ch, y, x], out.at[:, (y * 4 + x) * 2 + ch], out_send.at[ch, 0])

    def out_arrival(ch, r):
        y_from, x_from = (y + 4 - r // 4) % 4, (x + 4 - r % 4) % 4
        return pltpu.make_async_remote_copy(
            src_ref=staged.at[ch, y, x], dst_ref=out.at[:, (y_from * 4 + x_from) * 2 + ch],
            send_sem=out_send.at[ch, r], recv_sem=out_recv.at[ch, r],
            device_id=device(y_from, x_from), device_id_type=MESH)

    half_at = pl.multiple_of((z_hi % 2) * PADDED, PADDED)
    row = lax.broadcasted_iota(jnp.int32, (128, PADDED), 0)
    lane = lax.broadcasted_iota(jnp.int32, (128, PADDED), 1)
    pick = jnp.where((lane == row + ROWS * core) & (row < ROWS), 1.0, 0.0).astype(jnp.bfloat16)

    in_half = lax.broadcasted_iota(jnp.int32, (256, PADDED), 1) < HALF

    def prepare(q):
        ch, j = q // 4, panel(q)
        first = gathered[ch, j, z_hi // 2, :, :, :, pl.ds(half_at, PADDED)].reshape(32, 2, 16, PADDED)
        turned = jnp.stack([first[:, 1], -first[:, 0]], axis=1)
        upper = lax.dot_general(pick, first.reshape(1024, PADDED), (((1,), (1,)), ((), ())),
                                preferred_element_type=jnp.float32)
        lower = lax.dot_general(pick, turned.reshape(1024, PADDED), (((1,), (1,)), ((), ())),
                                preferred_element_type=jnp.float32)
        left[ch, j, :128] = upper.astype(jnp.bfloat16)
        left[ch, j, 128:] = lower.astype(jnp.bfloat16)
        row_power = jnp.sum(upper * upper, axis=1, keepdims=True) / SAMPLES + EPSILON
        scale = lax.rsqrt(row_power) * (1.0 / SAMPLES)
        left_scale[ch, j, :128] = scale
        left_scale[ch, j, 128:] = scale
        second = gathered[ch, j, z_lo].reshape(1024, WIDE).astype(jnp.float32)
        power = jnp.sum(second * second, axis=0, keepdims=True) / SAMPLES + EPSILON
        right_scale[ch, j] = lax.rsqrt(power)

    def unit(ch, i, j):
        right = gathered[ch, j, z_lo].reshape(1024, WIDE)
        product = jnp.dot(left[ch, i], right, preferred_element_type=jnp.float32)
        product = product * left_scale[ch, i] * right_scale[ch, j]
        upper = pltpu.roll(product[:, PADDED:], HALF, 1)
        lower = jnp.where(in_half, product[:, :PADDED], upper).astype(jnp.bfloat16)
        upper = upper.astype(jnp.bfloat16)
        for k in range(2):
            rows = slice(128 * k, 128 * k + ROWS)
            staged[ch, i, j, k, :, :PADDED] = lower[rows]
            staged[ch, i, j, k, :, PADDED:] = upper[rows, :COLUMNS - PADDED]
        r = ((i + 4 - y) % 4) * 4 + (j + 4 - x) % 4

        @pl.when(r == 0)
        def _():
            out_local(ch).start()

        @pl.when(r != 0)
        def _():
            out_remote(ch, i, j, r).start()

    def units(begin, end):
        def body(n, _):
            ch = n // 16
            at = choose(n // 8, orders) >> (4 * (n % 8))
            unit(ch, panel((at // 4) % 4), panel(at % 4))
            return 0

        lax.fori_loop(begin, end, body, 0)

    def in_wait(ch):
        in_local(ch).wait()
        for r in order:
            in_arrival(ch, r).wait_recv()

    def step(t, _):
        for ch in range(2):
            @pl.when(t == ch * 4)
            def _(ch=ch):
                in_wait(ch)

        @pl.when(t >= 2)
        def _():
            for part in range(2):
                for way in range(2):
                    ring_in(t - 2, HOPS, way, part).wait_recv()
            swap(t - 2, core).start()

        for part in range(2):
            @pl.when(t < 8)
            def _(part=part):
                send_hop(t, 1, part)

            @pl.when((t >= 1) & (t < 9))
            def _(part=part):
                send_hop(t - 1, 3, part)

        @pl.when(t == 1)
        def _():
            in_start(1)

        @pl.when(t >= 3)
        def _():
            units(choose(t, (0,) + END[:-1]), choose(t, MIDDLE))

        for part in range(2):
            @pl.when(t < 8)
            def _(part=part):
                send_hop(t, 2, part)

            @pl.when((t >= 1) & (t < 9))
            def _(part=part):
                send_hop(t - 1, 4, part)

        @pl.when(t >= 2)
        def _():
            swap(t - 2, 1 - core).wait_recv()
            prepare(t - 2)

        units(choose(t, MIDDLE), choose(t, END))
        return 0

    lax.fori_loop(0, 10, step, 0)

    def drain_ring(q, _):
        for way in range(2):
            for hop in range(1, HOPS + 1):
                for part in range(2):
                    ring_out(q, hop, way, part).wait_send()
        swap(q, core).wait_send()
        return 0

    lax.fori_loop(0, 8, drain_ring, 0)
    for ch in range(2):
        for r in range(1, 16):
            in_remote(ch, r).wait_send()

    def drain_out(r, _):
        y_to, x_to = partner(r)
        for ch in range(2):
            out_remote(ch, y_to, x_to, r).wait_send()
            out_arrival(ch, r).wait_recv()
        return 0

    lax.fori_loop(1, 16, drain_out, 0)
    for ch in range(2):
        out_local(ch).wait()


def exchange_rows(by_channel, by_row):
    by_row[0] = jnp.swapaxes(by_channel[0], 0, 1)


def per_device(voltages):
    parts, samples, channels, width = voltages.shape
    volts = jnp.transpose(voltages, (2, 0, 1, 3)).reshape(channels, parts * samples, width)
    gap = jnp.zeros((channels, parts * samples, PADDED - HALF), volts.dtype)
    volts = jnp.concatenate([volts[:, :, :HALF], gap, volts[:, :, HALF:], gap], axis=2)
    volts = volts.reshape(channels // 2, 2, parts * samples, WIDE)
    dma = pltpu.SemaphoreType.DMA
    out = pl.pallas_call(
        kernel,
        name="correlate",
        out_shape=jax.ShapeDtypeStruct((2, channels, ROWS, COLUMNS), jnp.bfloat16),
        in_specs=[pl.BlockSpec(memory_space=pltpu.VMEM)],
        out_specs=pl.BlockSpec(memory_space=pl.ANY),
        scratch_shapes=[
            pltpu.VMEM((2, 4, 2, 4, 2, 128, WIDE), jnp.bfloat16),
            pltpu.VMEM((2, 4, 256, 1024), jnp.bfloat16),
            pltpu.VMEM((2, 4, 256, 1), jnp.float32),
            pltpu.VMEM((2, 4, 1, WIDE), jnp.float32),
            pltpu.VMEM((2, 4, 4, 2, ROWS, COLUMNS), jnp.bfloat16),
            dma((2, 16)), dma((2, 16)),
            dma((8, 2, HOPS, 2)), dma((8, 2, HOPS, 2)),
            dma((8,)), dma((8,)),
            dma((2, 16)), dma((2, 16)),
        ],
        compiler_params=pltpu.CompilerParams(
            collective_id=0, has_side_effects=True, vmem_limit_bytes=48 << 20),
        cost_estimate=pl.CostEstimate(
            flops=2 * 32 * 256 * 1024 * 512, bytes_accessed=9 << 20, transcendentals=0),
    )(volts)
    out = pl.pallas_call(
        exchange_rows,
        name="exchange_rows",
        grid=(2, 2),
        in_specs=[pl.BlockSpec((1, channels, 64, COLUMNS), lambda k, i: (k, 0, i, 0))],
        out_specs=pl.BlockSpec((1, 64, channels, COLUMNS), lambda k, i: (k, i, 0, 0)),
        out_shape=jax.ShapeDtypeStruct((2, ROWS, channels, COLUMNS), jnp.bfloat16),
        compiler_params=pltpu.CompilerParams(vmem_limit_bytes=48 << 20),
    )(out)
    return jnp.swapaxes(out, 1, 2)


def solution(mesh):
    return jax.shard_map(
        per_device,
        mesh=mesh,
        in_specs=(P(None, "chan", None, "inp"),),
        out_specs=P(None, None, "chan", "inp"),
        check_vma=False,
    )
```

```python
import functools

import jax
import jax.numpy as jnp
from jax import lax
from jax.experimental import pallas as pl
from jax.experimental.pallas import tpu as pltpu
from jax.sharding import PartitionSpec as P

SAMPLES = 512
EPSILON = 1e-06
MESH = pl.DeviceIdType.MESH
ROWS = 125
COLUMNS = 500
HALF, PADDED = 250, 256
WIDE = 2 * PADDED
PANELS = ("0213", "0132", "1302", "0321")
EARLY = ("045189a26cdef37b", "015426a8937bfcde")
LATE = (
    ("82c3af41be596d70", "c506d287e1bf93a4", "6c2d41af50b7839e", "078539c61be2fad4"),
    ("c382fa41eb5d7960", "06c52d871eb3af94", "2d6c14af05b3978e", "850793c6b1ead2f4"),
)
MIDDLE = (0, 0, 0, 1, 4, 9, 13, 16, 16, 16)
END = (0, 0, 1, 4, 7, 11, 15, 16, 16, 32)
HOPS = 4


def word(digits, bits):
    packed = sum(int(digit, 16) << (bits * k) for k, digit in enumerate(digits))
    return packed - (1 << 32) if packed >= 1 << 31 else packed


def choose(at, values):
    chosen = jnp.int32(values[0])
    for k, value in enumerate(values[1:], 1):
        chosen = jnp.where(at == k, jnp.int32(value), chosen)
    return chosen


def kernel(volts, out, gathered, left, left_scale, right_scale, staged,
           in_send, in_recv, ring_send, ring_recv, swap_send, swap_recv, out_send, out_recv):
    chan, inp = lax.axis_index("chan"), lax.axis_index("inp")
    y, z_hi, core = chan // 8, (chan // 2) % 4, chan % 2
    x, z_lo = inp // 2, inp % 2
    z = z_hi * 2 + z_lo

    def device(y_to, x_to):
        return ((y_to * 4 + z_hi) * 2 + core, x_to * 2 + z_lo)

    def along_z(z_to):
        return ((y * 4 + z_to // 2) * 2 + core, x * 2 + z_to % 2)

    def partner(r):
        return (y + r // 4) % 4, (x + r % 4) % 4

    other_core = (chan + 1 - 2 * core, inp)

    barrier = pltpu.get_barrier_semaphore()
    for r in range(1, 16):
        pl.semaphore_signal(barrier, inc=1, device_id=device(*partner(r)), device_id_type=MESH)
    for to in (along_z((z + 1) % 8), along_z((z + 7) % 8), other_core):
        pl.semaphore_signal(barrier, inc=1, device_id=to, device_id_type=MESH)
    pl.semaphore_wait(barrier, 18)

    def in_copy(ch, r):
        y_to, x_to = partner(r)
        src = volts.at[y_to * 4 + x_to, ch]
        dst = gathered.at[ch, x, z_lo, z_hi, core, pl.ds(pl.multiple_of(y * 32, 32), 32)]
        return src, dst, device(y_to, x_to)

    def in_remote(ch, r):
        src, dst, to = in_copy(ch, r)
        return pltpu.make_async_remote_copy(
            src_ref=src, dst_ref=dst, send_sem=in_send.at[ch, r], recv_sem=in_recv.at[ch, r],
            device_id=to, device_id_type=MESH)

    def in_arrival(ch, r):
        y_from, x_from = (y + 4 - r // 4) % 4, (x + 4 - r % 4) % 4
        dst = gathered.at[ch, x_from, z_lo, z_hi, core, pl.ds(pl.multiple_of(y_from * 32, 32), 32)]
        return pltpu.make_async_remote_copy(
            src_ref=dst, dst_ref=dst, send_sem=in_send.at[ch, r], recv_sem=in_recv.at[ch, r],
            device_id=device(y_from, x_from), device_id_type=MESH)

    def in_local(ch):
        src, dst, _ = in_copy(ch, 0)
        return pltpu.make_async_copy(src, dst, in_send.at[ch, 0])

    order = (5, 15, 7, 13, 10, 1, 4, 3, 12, 2, 8, 6, 9, 14, 11)
    def in_start(ch):
        in_local(ch).start()
        for r in order:
            in_remote(ch, r).start()

    in_start(0)

    case = (y + 4 - x) % 4
    panels = choose(case, [word(p, 2) for p in PANELS])
    orders = [choose(core, [word(o[h:h + 8], 4) for o in EARLY]) for h in (0, 8)]
    orders += [choose(core * 4 + case, [word(o[h:h + 8], 4) for row in LATE for o in row]) for h in (0, 8)]

    def panel(q):
        return (x + (panels >> (2 * (q % 4))) % 4) % 4

    def piece(q, source, hop, way, part):
        whole = gathered.at[q // 4, panel(q), source % 2, source // 2, core, pl.ds(64 * part, 64)]
        if hop < 3:
            return whole
        half = ((source + 1) // 2 + 1 + way) % 2
        return whole.at[:, pl.ds(pl.multiple_of(half * PADDED, PADDED), PADDED)]

    def ring_copy(q, hop, way, part, source):
        ref = piece(q, source, hop, way, part)
        to = along_z((z + (1 if way == 0 else 7)) % 8)
        return pltpu.make_async_remote_copy(
            src_ref=ref, dst_ref=ref, send_sem=ring_send.at[q, way, hop - 1, part],
            recv_sem=ring_recv.at[q, way, hop - 1, part], device_id=to, device_id_type=MESH)

    def ring_out(q, hop, way, part):
        source = (z + (9 - hop if way == 0 else hop - 1)) % 8
        return ring_copy(q, hop, way, part, source)

    def ring_in(q, hop, way, part):
        source = (z + (8 - hop if way == 0 else hop)) % 8
        return ring_copy(q, hop, way, part, source)

    def send_hop(q, hop, part):
        for way in range(2):
            if hop > 1:
                ring_in(q, hop - 1, way, part).wait_recv()
            ring_out(q, hop, way, part).start()

    def swap(q, own):
        ref = gathered.at[q // 4, panel(q), :, :, own]
        return pltpu.make_async_remote_copy(
            src_ref=ref, dst_ref=ref, send_sem=swap_send.at[q], recv_sem=swap_recv.at[q],
            device_id=other_core, device_id_type=MESH)

    def out_remote(ch, i, j, r):
        return pltpu.make_async_remote_copy(
            src_ref=staged.at[ch, i, j], dst_ref=out.at[:, (y * 4 + x) * 2 + ch],
            send_sem=out_send.at[ch, r], recv_sem=out_recv.at[ch, r],
            device_id=device(i, j), device_id_type=MESH)

    def out_local(ch):
        return pltpu.make_async_copy(
            staged.at[ch, y, x], out.at[:, (y * 4 + x) * 2 + ch], out_send.at[ch, 0])

    def out_arrival(ch, r):
        y_from, x_from = (y + 4 - r // 4) % 4, (x + 4 - r % 4) % 4
        return pltpu.make_async_remote_copy(
            src_ref=staged.at[ch, y, x], dst_ref=out.at[:, (y_from * 4 + x_from) * 2 + ch],
            send_sem=out_send.at[ch, r], recv_sem=out_recv.at[ch, r],
            device_id=device(y_from, x_from), device_id_type=MESH)

    half_at = pl.multiple_of((z_hi % 2) * PADDED, PADDED)
    row = lax.broadcasted_iota(jnp.int32, (128, PADDED), 0)
    lane = lax.broadcasted_iota(jnp.int32, (128, PADDED), 1)
    pick = jnp.where((lane == row + ROWS * core) & (row < ROWS), 1.0, 0.0).astype(jnp.bfloat16)

    in_half = lax.broadcasted_iota(jnp.int32, (256, PADDED), 1) < HALF

    def prepare(q):
        ch, j = q // 4, panel(q)
        first = gathered[ch, j, z_hi // 2, :, :, :, pl.ds(half_at, PADDED)].reshape(32, 2, 16, PADDED)
        turned = jnp.stack([first[:, 1], -first[:, 0]], axis=1)
        upper = lax.dot_general(pick, first.reshape(1024, PADDED), (((1,), (1,)), ((), ())),
                                preferred_element_type=jnp.float32)
        lower = lax.dot_general(pick, turned.reshape(1024, PADDED), (((1,), (1,)), ((), ())),
                                preferred_element_type=jnp.float32)
        left[ch, j, :128] = upper.astype(jnp.bfloat16)
        left[ch, j, 128:] = lower.astype(jnp.bfloat16)
        row_power = jnp.sum(upper * upper, axis=1, keepdims=True) / SAMPLES + EPSILON
        scale = lax.rsqrt(row_power) * (1.0 / SAMPLES)
        left_scale[ch, j, :128] = scale
        left_scale[ch, j, 128:] = scale
        second = gathered[ch, j, z_lo].reshape(1024, WIDE).astype(jnp.float32)
        power = jnp.sum(second * second, axis=0, keepdims=True) / SAMPLES + EPSILON
        right_scale[ch, j] = lax.rsqrt(power)

    def unit(ch, i, j):
        right = gathered[ch, j, z_lo].reshape(1024, WIDE)
        product = jnp.dot(left[ch, i], right, preferred_element_type=jnp.float32)
        product = product * left_scale[ch, i] * right_scale[ch, j]
        upper = pltpu.roll(product[:, PADDED:], HALF, 1)
        lower = jnp.where(in_half, product[:, :PADDED], upper).astype(jnp.bfloat16)
        upper = upper.astype(jnp.bfloat16)
        for k in range(2):
            rows = slice(128 * k, 128 * k + ROWS)
            staged[ch, i, j, k, :, :PADDED] = lower[rows]
            staged[ch, i, j, k, :, PADDED:] = upper[rows, :COLUMNS - PADDED]
        r = ((i + 4 - y) % 4) * 4 + (j + 4 - x) % 4

        @pl.when(r == 0)
        def _():
            out_local(ch).start()

        @pl.when(r != 0)
        def _():
            out_remote(ch, i, j, r).start()

    def units(begin, end):
        def body(n, _):
            ch = n // 16
            at = choose(n // 8, orders) >> (4 * (n % 8))
            unit(ch, panel((at // 4) % 4), panel(at % 4))
            return 0

        lax.fori_loop(begin, end, body, 0)

    def in_wait(ch):
        in_local(ch).wait()
        for r in order:
            in_arrival(ch, r).wait_recv()

    def step(t, _):
        for ch in range(2):
            @pl.when(t == ch * 4)
            def _(ch=ch):
                in_wait(ch)

        @pl.when(t >= 2)
        def _():
            for part in range(2):
                for way in range(2):
                    ring_in(t - 2, HOPS, way, part).wait_recv()
            swap(t - 2, core).start()

        for part in range(2):
            @pl.when(t < 8)
            def _(part=part):
                send_hop(t, 1, part)

            @pl.when((t >= 1) & (t < 9))
            def _(part=part):
                send_hop(t - 1, 3, part)

        @pl.when(t == 1)
        def _():
            in_start(1)

        @pl.when(t >= 3)
        def _():
            units(choose(t, (0,) + END[:-1]), choose(t, MIDDLE))

        for part in range(2):
            @pl.when(t < 8)
            def _(part=part):
                send_hop(t, 2, part)

            @pl.when((t >= 1) & (t < 9))
            def _(part=part):
                send_hop(t - 1, 4, part)

        @pl.when(t >= 2)
        def _():
            swap(t - 2, 1 - core).wait_recv()
            prepare(t - 2)

        units(choose(t, MIDDLE), choose(t, END))
        return 0

    lax.fori_loop(0, 10, step, 0)

    def drain_ring(q, _):
        for way in range(2):
            for hop in range(1, HOPS + 1):
                for part in range(2):
                    ring_out(q, hop, way, part).wait_send()
        swap(q, core).wait_send()
        return 0

    lax.fori_loop(0, 8, drain_ring, 0)
    for ch in range(2):
        for r in range(1, 16):
            in_remote(ch, r).wait_send()

    def drain_out(r, _):
        y_to, x_to = partner(r)
        for ch in range(2):
            out_remote(ch, y_to, x_to, r).wait_send()
            out_arrival(ch, r).wait_recv()
        return 0

    lax.fori_loop(1, 16, drain_out, 0)
    for ch in range(2):
        out_local(ch).wait()


def exchange_rows(by_channel, by_row):
    by_row[0] = jnp.swapaxes(by_channel[0], 0, 1)


def per_device(voltages):
    parts, samples, channels, width = voltages.shape
    volts = jnp.transpose(voltages, (2, 0, 1, 3)).reshape(channels, parts * samples, width)
    gap = jnp.zeros((channels, parts * samples, PADDED - HALF), volts.dtype)
    volts = jnp.concatenate([volts[:, :, :HALF], gap, volts[:, :, HALF:], gap], axis=2)
    volts = volts.reshape(channels // 2, 2, parts * samples, WIDE)
    dma = pltpu.SemaphoreType.DMA
    out = pl.pallas_call(
        kernel,
        name="correlate",
        out_shape=jax.ShapeDtypeStruct((2, channels, ROWS, COLUMNS), jnp.bfloat16),
        in_specs=[pl.BlockSpec(memory_space=pltpu.VMEM)],
        out_specs=pl.BlockSpec(memory_space=pl.ANY),
        scratch_shapes=[
            pltpu.VMEM((2, 4, 2, 4, 2, 128, WIDE), jnp.bfloat16),
            pltpu.VMEM((2, 4, 256, 1024), jnp.bfloat16),
            pltpu.VMEM((2, 4, 256, 1), jnp.float32),
            pltpu.VMEM((2, 4, 1, WIDE), jnp.float32),
            pltpu.VMEM((2, 4, 4, 2, ROWS, COLUMNS), jnp.bfloat16),
            dma((2, 16)), dma((2, 16)),
            dma((8, 2, HOPS, 2)), dma((8, 2, HOPS, 2)),
            dma((8,)), dma((8,)),
            dma((2, 16)), dma((2, 16)),
        ],
        compiler_params=pltpu.CompilerParams(
            collective_id=0, has_side_effects=True, vmem_limit_bytes=48 << 20),
        cost_estimate=pl.CostEstimate(
            flops=2 * 32 * 256 * 1024 * 512, bytes_accessed=9 << 20, transcendentals=0),
    )(volts)
    out = pl.pallas_call(
        exchange_rows,
        name="exchange_rows",
        grid=(2, 1),
        in_specs=[pl.BlockSpec((1, channels, ROWS, COLUMNS), lambda k, i: (k, 0, i, 0))],
        out_specs=pl.BlockSpec((1, ROWS, channels, COLUMNS), lambda k, i: (k, i, 0, 0)),
        out_shape=jax.ShapeDtypeStruct((2, ROWS, channels, COLUMNS), jnp.bfloat16),
        compiler_params=pltpu.CompilerParams(vmem_limit_bytes=48 << 20),
    )(out)
    return jnp.swapaxes(out, 1, 2)


def solution(mesh):
    return jax.shard_map(
        per_device,
        mesh=mesh,
        in_specs=(P(None, "chan", None, "inp"),),
        out_specs=P(None, None, "chan", "inp"),
        check_vma=False,
    )
```
